256 devices in a mesh: gx: 16 (over y_hi, x, core), gy: 16 (over y_lo, z).
Axes of the slice: x: 4, y: 4 (y_hi: 2, y_lo: 2; y = y_hi * 2 + y_lo), z: 8, core: 2. Of those that a mesh axis runs over, the one named last changes fastest.
Arguments:
- subspace: bfloat16 [16, 16, 2048, 256], P('gx', 'gy'), may hold values from -200 to 200
- hamiltonian: bfloat16 [16, 16, 32, 64, 512], P('gx', 'gy'), may hold values from -0.125 to 0.125
- neighbours: int32 [16, 16, 32, 8], P('gx', 'gy'), may hold values from 0 to 39
- send_lists: int32 [16, 16, 4, 2], P('gx', 'gy'), may hold values from 0 to 31
- rotation: bfloat16 [256, 256], replicated, may hold values from -0.375 to 0.375
Outputs:
- rotated: bfloat16 [16, 16, 2048, 256], P('gx', 'gy')
- margin: float32 [256, 256], P(('gx', 'gy'))
The draws below stay inside these ranges and needn't reach their ends.
Inputs may be any that keep to these rules, and one draw needn't show every extreme that they name: `neighbours`: slots below 32 are the device's own blocks; slot 32 + d * 2 + h is the h-th block of packet d received.
All inputs are finite; a program needn't handle non-finite values.
Results may differ from the reference program's by a relative error of at most 0.013.
Values may be sent and summed in bfloat16 or wider, within the bound.
No kernel may reach another device: no remote copies, remote signals or barrier semaphores. Data moves between devices by JAX's collectives and lax.ppermute only.
A program may use at most 64 MiB of HBM per device.

```python
import math
import jax
import jax.numpy as jnp
from jax import lax

ORB = 64
SUB = 256
NB = 8
HB = 2
STEPS = 6
BLK_DEV = 32
TILES_X = 16
TILES_Y = 16
ROWS_DEV = 2048
ORBITALS = 524288


def draw_subspace(key, part):
    key = jax.random.fold_in(key, 17)
    base_key, row_key, column_key = jax.random.split(key, 3)
    shape = (TILES_X, TILES_Y, ROWS_DEV, SUB)
    row_scale = jnp.exp(jax.random.uniform(row_key, (TILES_X, TILES_Y, ROWS_DEV, 1), jnp.float32, math.log(0.3), math.log(3.0)))
    column_scale = jnp.exp(jax.random.uniform(column_key, (1, 1, 1, SUB), jnp.float32, math.log(0.3), math.log(3.0)))
    tile_number = jnp.arange(TILES_X * TILES_Y, dtype=jnp.float32).reshape(TILES_X, TILES_Y, 1, 1)
    ramp = 1.0 + 2.0 * tile_number / max(TILES_X * TILES_Y - 1, 1)
    base = jax.random.normal(base_key, shape, jnp.float32)
    return (base * row_scale * column_scale * ramp).astype(jnp.bfloat16)


def plant(entries, own_key, smallest, top_value):
    longest = entries.shape.index(max(entries.shape))
    spots = []
    for shift in (0, 1):
        where = [jax.random.randint(jax.random.fold_in(own_key, axis), (), 0, length) for axis, length in enumerate(entries.shape)]
        where[longest] = (where[longest] + shift) % entries.shape[longest]
        spots.append(tuple(where))
    return entries.at[spots[0]].set(smallest).at[spots[1]].set(top_value)


def levels(stream_key, dims, cuts, smallest, top_value):
    def one(axis_at, shards_of):
        steps = jax.random.uniform(jax.random.fold_in(jax.random.fold_in(stream_key, 6), axis_at), (shards_of,), jnp.float32, smallest / len(cuts), top_value / len(cuts))
        return jnp.repeat(jnp.exp(steps), dims[axis_at] // shards_of).reshape((-1,) + (1,) * (len(dims) - axis_at - 1))

    loudness = one(*cuts[0])
    for cut in cuts[1:]:
        loudness = loudness * one(*cut)
    return loudness


def gaussian(own_key, dims, scale, most, shards=(), kind=jnp.bfloat16):
    drawn = jax.random.normal(own_key, dims, jnp.float32) * scale
    if len(shards) > 0:
        drawn = levels(own_key, dims, shards, -0.22, 0.18) * drawn
    return jnp.clip(drawn, min=-most, max=most).astype(kind)


def setup_inputs(seed: int = 0) -> dict:
    arg_keys = jax.random.split(jax.random.key(seed), 6)
    return {
        "subspace": draw_subspace(jax.random.fold_in(arg_keys[5], 71), 0),
        "hamiltonian": gaussian(arg_keys[1], (TILES_X, TILES_Y, BLK_DEV, ORB, NB * ORB), (4 * NB * ORB) ** -0.5, 0.125, ((0, 16), (1, 16))),
        "neighbours": plant(jax.random.randint(arg_keys[2], (TILES_X, TILES_Y, BLK_DEV, NB), 0, BLK_DEV + 4 * HB), jax.random.fold_in(arg_keys[2], 1), 0, (BLK_DEV + 4 * HB) - 1).astype(jnp.int32),
        "send_lists": plant(jax.random.randint(arg_keys[3], (TILES_X, TILES_Y, 4, HB), 0, BLK_DEV), jax.random.fold_in(arg_keys[3], 1), 0, BLK_DEV - 1).astype(jnp.int32),
        "rotation": gaussian(arg_keys[4], (SUB, SUB), SUB ** -0.5, 0.375),
    }


center_shift = 0.1
half_width = 0.8


def pick_packets(lowered, outgoing):
    return lowered[outgoing.reshape(-1)].reshape(4, HB, ORB, SUB)


def one_tile(inputs):
    table, coupling, link = inputs
    gathered = table[link].reshape(BLK_DEV, NB * ORB, SUB)
    return jnp.einsum("rak,rkc->rac", coupling.astype(jnp.float32), gathered.astype(jnp.float32))


def reference(subspace, hamiltonian, neighbours, send_lists, rotation):
    tiles = TILES_X * TILES_Y
    couplings = hamiltonian.reshape(tiles, BLK_DEV, ORB, NB * ORB)
    links = neighbours.reshape(tiles, BLK_DEV, NB)

    def scaled_apply(state):
        lowered = state.astype(jnp.bfloat16)
        packets = jax.vmap(jax.vmap(pick_packets))(lowered, send_lists)
        edge_x = jnp.zeros((1, TILES_Y, HB, ORB, SUB), jnp.bfloat16)
        edge_y = jnp.zeros((TILES_X, 1, HB, ORB, SUB), jnp.bfloat16)
        from_prev_x = jnp.concatenate([edge_x, packets[:-1, :, 0]], axis=0)
        from_next_x = jnp.concatenate([packets[1:, :, 1], edge_x], axis=0)
        from_prev_y = jnp.concatenate([edge_y, packets[:, :-1, 2]], axis=1)
        from_next_y = jnp.concatenate([packets[:, 1:, 3], edge_y], axis=1)
        extended = jnp.concatenate([lowered, from_prev_x, from_next_x, from_prev_y, from_next_y], axis=2)
        product = lax.map(one_tile, (extended.reshape(tiles, BLK_DEV + 4 * HB, ORB, SUB), couplings, links))
        return (product.reshape(state.shape) - center_shift * state) / half_width

    start_state = subspace.astype(jnp.float32).reshape(TILES_X, TILES_Y, BLK_DEV, ORB, SUB)
    previous = start_state
    present = scaled_apply(start_state)
    for degree in range(STEPS - 1):
        following = 2.0 * scaled_apply(present) - previous
        previous, present = present, following
    filtered = present.astype(jnp.bfloat16).reshape(ORBITALS, SUB)
    gram = jnp.dot(filtered.T, filtered, preferred_element_type=jnp.float32)
    rotated = jnp.dot(filtered, rotation, preferred_element_type=jnp.float32).astype(jnp.bfloat16)
    rotated = rotated.reshape(TILES_X, TILES_Y, ROWS_DEV, SUB)
    rotation_wide = rotation.astype(jnp.float32)
    right_side = jnp.dot(gram, rotation_wide, precision=lax.Precision.HIGHEST)
    margin = jnp.dot(rotation_wide.T, right_side, precision=lax.Precision.HIGHEST) / ORBITALS
    return rotated, margin
```

```python
import functools

import jax
import jax.numpy as jnp
from jax import lax
from jax.experimental import pallas as pl
from jax.experimental.pallas import tpu as pltpu
from jax.sharding import PartitionSpec as P

STEPS = 6
SHIFT = 0.1
HALF_WIDTH = 0.8

F32 = jnp.float32
BF16 = jnp.bfloat16
VMEM = pltpu.VMEM
SMEM = pltpu.SMEM

ORB = 64
NB = 8
BLK = 32
HB = 2
ROWS = BLK * ORB
SUB = 256
HALO = 4 * HB * ORB
WIDE = ROWS + HALO + 2 * ORB
SPARE = BLK + 4 * HB
MT = 512


def exchange_pairs(tiles_x, tiles_y):
    def at(i, j):
        return i * tiles_y + j

    def odd(i):
        return ((i - 1) ^ 1) + 1

    grid = [(i, j) for i in range(tiles_x) for j in range(tiles_y)]
    inner_x = [(at(i, j), at(i ^ 1, j)) for i, j in grid]
    inner_y = [(at(i, j), at(i, j ^ 1)) for i, j in grid]
    outer_x = [
        (at(i, j), at(i, j ^ 1) if i in (0, tiles_x - 1) else at(odd(i), j)) for i, j in grid
    ]
    outer_y = [
        (at(i, j), at(i ^ 1, j) if j in (0, tiles_y - 1) else at(i, odd(j))) for i, j in grid
    ]
    return inner_x, outer_x, inner_y, outer_y


def dot(a, b):
    return jnp.dot(a, b, preferred_element_type=F32)


def build_kernel(place, nbr, ham, sub, dense, base, cur, remap):
    for s in range(BLK):
        remap[s] = jnp.int32(s)
    for axis in range(2):
        pos, last = place[axis], place[2 + axis]
        parity = pos & 1
        for side in range(2):
            exists = (pos > 0) if side == 0 else (pos < last)
            op = jnp.where(parity == side, 1, 0) if side == 0 else jnp.where(parity == 0, 0, 1)
            for h in range(HB):
                s = BLK + (2 * axis + side) * HB + h
                remap[s] = jnp.where(exists, BLK + (2 * axis + op) * HB + h, SPARE)

    def clear(m, carry):
        dense[pl.ds(pl.multiple_of(m * ORB, ORB), ORB), :] = jnp.zeros((ORB, WIDE), BF16)
        return carry

    lax.fori_loop(0, BLK, clear, 0)
    low = lax.broadcasted_iota(jnp.int32, (ORB, 2 * ORB), 1) < ORB

    def row(r, carry):
        rows = pl.ds(pl.multiple_of(r * ORB, ORB), ORB)
        for kk in range(NB // 2):
            tile = ham[rows, kk * 128:(kk + 1) * 128].astype(F32)
            turned = pltpu.roll(tile, 64, 1)
            for e in range(2):
                s = remap[nbr[r, 2 * kk + e]]
                p = s & 1
                q = s >> 1
                high_part = jnp.where(low, 0.0, tile if e == 1 else turned)
                low_part = jnp.where(low, tile if e == 0 else turned, 0.0)
                piece = jnp.where(p == 0, low_part, high_part)
                cols = pl.ds(pl.multiple_of(q * 128, 128), 128)
                dense[rows, cols] = (dense[rows, cols].astype(F32) + piece).astype(BF16)
        return carry

    lax.fori_loop(0, BLK, row, 0)

    def local(m, carry):
        rows = pl.ds(pl.multiple_of(m * MT, MT), MT)
        wide = sub[rows, :].astype(F32)
        cur[rows, :] = wide
        product = dot(dense[rows, :ROWS], sub[...])
        base[rows, :] = (1.0 / HALF_WIDTH) * product - (SHIFT / HALF_WIDTH) * wide
        return carry

    lax.fori_loop(0, ROWS // MT, local, 0, unroll=True)


def first_packets_kernel(place, lists, sub, out_a, out_b, out_c, out_d):
    for n, out in enumerate((out_a, out_b, out_c, out_d)):
        parity = place[n // 2] & 1
        packet = 2 * (n // 2) + ((parity + n) & 1)
        for h in range(HB):
            b = lists[packet, h]
            out[h * ORB:(h + 1) * ORB, :] = sub[pl.ds(pl.multiple_of(b * ORB, ORB), ORB), :]


def packets_kernel(scale, place, lists, in_a, in_b, in_c, in_d, dense, base,
                   out_a, out_b, out_c, out_d, halo, rows_of, start):
    for n, got in enumerate((in_a, in_b, in_c, in_d)):
        halo[n * 2 * ORB:(n + 1) * 2 * ORB, :] = got[...]
    for n in range(4):
        parity = place[n // 2] & 1
        packet = 2 * (n // 2) + ((parity + n) & 1)
        for h in range(HB):
            at = pl.ds(pl.multiple_of(lists[packet, h] * ORB, ORB), ORB)
            here = slice((n * HB + h) * ORB, (n * HB + h + 1) * ORB)
            rows_of[here, :] = dense[at, ROWS:ROWS + HALO]
            start[here, :] = base[at, :]
    for n, out in enumerate((out_a, out_b, out_c, out_d)):
        here = slice(n * 2 * ORB, (n + 1) * 2 * ORB)
        out[...] = (start[here, :] + scale * dot(rows_of[here, :], halo[...])).astype(BF16)


def step_kernel(scale, in_a, in_b, in_c, in_d, dense, base, cur, new_cur, new_base, halo, low):
    for n, got in enumerate((in_a, in_b, in_c, in_d)):
        halo[n * 2 * ORB:(n + 1) * 2 * ORB, :] = got[...]

    def edge(m, carry):
        rows = pl.ds(pl.multiple_of(m * MT, MT), MT)
        value = base[rows, :] + scale * dot(dense[rows, ROWS:ROWS + HALO], halo[...])
        new_cur[rows, :] = value
        low[rows, :] = value.astype(BF16)
        return carry

    lax.fori_loop(0, ROWS // MT, edge, 0, unroll=True)

    def local(m, carry):
        rows = pl.ds(pl.multiple_of(m * MT, MT), MT)
        product = dot(dense[rows, :ROWS], low[...])
        new_base[rows, :] = (
            (2.0 / HALF_WIDTH) * product
            - (2.0 * SHIFT / HALF_WIDTH) * new_cur[rows, :]
            - cur[rows, :]
        )
        return carry

    lax.fori_loop(0, ROWS // MT, local, 0, unroll=True)


def last_kernel(scale, weight, in_a, in_b, in_c, in_d, dense, base, rotation, rotated, margin, halo, total):
    for n, got in enumerate((in_a, in_b, in_c, in_d)):
        halo[n * 2 * ORB:(n + 1) * 2 * ORB, :] = got[...]
    total[...] = jnp.zeros_like(total)

    def edge(m, carry):
        rows = pl.ds(pl.multiple_of(m * MT, MT), MT)
        value = base[rows, :] + scale * dot(dense[rows, ROWS:ROWS + HALO], halo[...])
        turned = dot(value.astype(BF16), rotation[...]).astype(BF16)
        rotated[rows, :] = turned
        total[...] += lax.dot_general(
            turned, turned, (((0,), (0,)), ((), ())), preferred_element_type=F32
        )
        return carry

    lax.fori_loop(0, ROWS // MT, edge, 0, unroll=True)
    margin[...] = (total[...] * weight).astype(BF16)


def params(**kw):
    return pltpu.CompilerParams(vmem_limit_bytes=16 * 1024 * 1024, **kw)


def cost(flops):
    return pl.CostEstimate(flops=int(flops), bytes_accessed=4 << 20, transcendentals=0)


V = pl.BlockSpec(memory_space=VMEM)
S = pl.BlockSpec(memory_space=SMEM)


def on_device(pairs, subspace, hamiltonian, neighbours, send_lists, rotation):
    ham = hamiltonian.reshape(ROWS, NB * ORB)
    nbr = neighbours.reshape(BLK, NB)
    lists = send_lists.reshape(4, HB)
    sub = subspace.reshape(ROWS, SUB)
    size_x, size_y = lax.axis_size("gx"), lax.axis_size("gy")
    place = jnp.stack([
        lax.axis_index("gx"), lax.axis_index("gy"), jnp.int32(size_x - 1), jnp.int32(size_y - 1)
    ]).astype(jnp.int32)

    packet = VMEM((2 * ORB, SUB), BF16)
    field = VMEM((ROWS, SUB), F32)
    halo = VMEM((HALO, SUB), BF16)

    def swap(packets):
        got = {}
        for n in (1, 3, 2, 0):
            got[n] = lax.ppermute(packets[n], ("gx", "gy"), pairs[n])
        return [got[n] for n in range(4)]

    packets = pl.pallas_call(
        first_packets_kernel,
        out_shape=[packet] * 4,
        in_specs=[S, S, V],
        out_specs=[V] * 4,
        compiler_params=params(),
        name="first_packets",
    )(place, lists, sub)
    received = swap(packets)
    dense, base, cur = pl.pallas_call(
        build_kernel,
        out_shape=[VMEM((ROWS, WIDE), BF16), field, field],
        in_specs=[S, S, V, V],
        out_specs=[V] * 3,
        scratch_shapes=[SMEM((SPARE + 8,), jnp.int32)],
        compiler_params=params(),
        cost_estimate=cost(2e9),
        name="build_and_local",
    )(place, nbr, ham, sub)
    for step in range(1, STEPS):
        scale = (1.0 if step == 1 else 2.0) / HALF_WIDTH
        packets = pl.pallas_call(
            functools.partial(packets_kernel, scale),
            out_shape=[packet] * 4,
            in_specs=[S, S] + [V] * 6,
            out_specs=[V] * 4,
            scratch_shapes=[halo, VMEM((HALO, HALO), BF16), VMEM((HALO, SUB), F32)],
            compiler_params=params(),
            name="packets",
        )(place, lists, *received, dense, base)
        landed = received
        received = swap(packets)
        cur, base = pl.pallas_call(
            functools.partial(step_kernel, scale),
            out_shape=[field, field],
            in_specs=[V] * 7,
            out_specs=[V] * 2,
            scratch_shapes=[halo, VMEM((ROWS, SUB), BF16)],
            compiler_params=params(),
            cost_estimate=cost(2.7e9),
            name="step",
        )(*landed, dense, base, cur)
    orbitals = ROWS * size_x * size_y
    rotated, share = pl.pallas_call(
        functools.partial(last_kernel, 2.0 / HALF_WIDTH, 1.0 / orbitals),
        out_shape=[jax.ShapeDtypeStruct((ROWS, SUB), BF16), VMEM((SUB, SUB), BF16)],
        in_specs=[V] * 7,
        out_specs=[V] * 2,
        scratch_shapes=[halo, VMEM((SUB, SUB), F32)],
        compiler_params=params(),
        name="last",
    )(*received, dense, base, rotation)
    parts = lax.all_to_all(share, ("gx", "gy"), 0, 0, tiled=True)
    margin = jnp.sum(parts.astype(F32), axis=0, keepdims=True)
    return rotated.reshape(subspace.shape), margin


def solution(mesh):
    pairs = exchange_pairs(mesh.shape["gx"], mesh.shape["gy"])
    return jax.shard_map(
        functools.partial(on_device, pairs),
        mesh=mesh,
        in_specs=(
            P("gx", "gy", None, None),
            P("gx", "gy", None, None, None),
            P("gx", "gy", None, None),
            P("gx", "gy", None, None),
            P(),
        ),
        out_specs=(P("gx", "gy", None, None), P(("gx", "gy"), None)),
        check_vma=False,
    )
```

```python
import functools

import jax
import jax.numpy as jnp
from jax import lax
from jax.experimental import pallas as pl
from jax.experimental.pallas import tpu as pltpu
from jax.sharding import PartitionSpec as P

STEPS = 6
SHIFT = 0.1
HALF_WIDTH = 0.8

F32 = jnp.float32
BF16 = jnp.bfloat16
VMEM = pltpu.VMEM
SMEM = pltpu.SMEM

ORB = 64
NB = 8
BLK = 32
HB = 2
ROWS = BLK * ORB
SUB = 256
HALO = 4 * HB * ORB
WIDE = ROWS + HALO + 2 * ORB
SPARE = BLK + 4 * HB
MT = 512
GROUP = 4


SWAPS = ((0, 1), (1, 1), (1, 0), (0, 0))


def exchange_pairs(tiles):
    grid = [(i, j) for i in range(tiles[0]) for j in range(tiles[1])]

    def partner(spot, axis, outer):
        place = list(spot)
        if outer and place[axis] in (0, tiles[axis] - 1):
            place[1 - axis] ^= 1
        else:
            place[axis] = ((place[axis] - outer) ^ 1) + outer
        return place[0] * tiles[1] + place[1]

    return [[(i * tiles[1] + j, partner((i, j), *swap)) for i, j in grid] for swap in SWAPS]


def dot(a, b):
    return jnp.dot(a, b, preferred_element_type=F32)


def build_kernel(meta, nbr, ham, sub, cleared, dense, base, cur, remap):
    for s in range(BLK):
        remap[s] = jnp.int32(s)
    for axis in range(2):
        pos, last = meta[axis], meta[2 + axis]
        even = (pos & 1) == 0
        inner, outer = SWAPS.index((axis, 0)), SWAPS.index((axis, 1))
        before, after = jnp.where(even, outer, inner), jnp.where(even, inner, outer)
        for h in range(HB):
            s = BLK + 2 * axis * HB + h
            remap[s] = jnp.where(pos > 0, BLK + before * HB + h, SPARE)
            remap[s + HB] = jnp.where(pos < last, BLK + after * HB + h, SPARE)

    low = lax.broadcasted_iota(jnp.int32, (ORB, 2 * ORB), 1) < ORB
    keep_low = jnp.where(low, 1.0, 0.0).astype(BF16)
    keep_high = jnp.where(low, 0.0, 1.0).astype(BF16)

    def group(g, carry):
        rows = [pl.ds(pl.multiple_of((g * GROUP + n) * ORB, ORB), ORB) for n in range(GROUP)]
        for kk in range(NB // 2):
            tiles = [ham[rows[n], kk * 128:(kk + 1) * 128] for n in range(GROUP)]
            turned = [pltpu.roll(tile, 64, 1) for tile in tiles]
            for e in range(2):
                spots, values = [], []
                for n in range(GROUP):
                    s = remap[nbr[2 * kk + e, g * GROUP + n]]
                    kept, moved = (keep_low, keep_high) if e == 0 else (keep_high, keep_low)
                    piece = jnp.where((s & 1) == e, tiles[n] * kept, turned[n] * moved)
                    spots.append((rows[n], pl.ds(pl.multiple_of((s >> 1) * 128, 128), 128)))
                    values.append(dense[spots[n]] + piece)
                for n in range(GROUP):
                    dense[spots[n]] = values[n]
        return carry

    lax.fori_loop(0, BLK // GROUP, group, 0)
    for m in range(ROWS // MT):
        rows = slice(m * MT, (m + 1) * MT)
        wide = sub[rows, :].astype(F32)
        cur[rows, :] = wide
        product = dot(dense[rows, :ROWS], sub[...])
        base[rows, :] = (1.0 / HALF_WIDTH) * product - (SHIFT / HALF_WIDTH) * wide


def sent_rows(meta, n, h):
    axis, outer = SWAPS[n]
    packet = 2 * axis + ((meta[axis] + outer) & 1)
    return pl.ds(pl.multiple_of(meta[4 + h * 4 + packet] * ORB, ORB), ORB)


def first_kernel(limits, lists, nbr_hbm, ham_hbm, sub_hbm, out_a, out_b, out_c, out_d, meta, nbr, ham, sub, dense, sems):
    for axis, name in enumerate(("gx", "gy")):
        meta[axis] = lax.axis_index(name)
        meta[2 + axis] = jnp.int32(limits[axis])
    for n in range(4):
        for h in range(HB):
            meta[4 + h * 4 + n] = lists[h, n]
    copies = []
    for n, out in enumerate((out_a, out_b, out_c, out_d)):
        for h in range(HB):
            copies.append((sub_hbm.at[sent_rows(meta, n, h), :], out.at[pl.ds(h * ORB, ORB), :]))
    copies += [(nbr_hbm, nbr), (ham_hbm, ham), (sub_hbm, sub)]
    copies = [pltpu.make_async_copy(*pair, sems.at[n]) for n, pair in enumerate(copies)]
    for copy in copies:
        copy.start()

    def clear(m, carry):
        dense[pl.ds(pl.multiple_of(m * ORB, ORB), ORB), :ROWS + HALO] = jnp.zeros((ORB, ROWS + HALO), BF16)
        return carry

    lax.fori_loop(0, BLK, clear, 0)
    for copy in copies:
        copy.wait()


def packets_kernel(scale, meta, in_a, in_b, in_c, in_d, dense, base, out_a, out_b, out_c, out_d):
    outs = (out_a, out_b, out_c, out_d)
    halo = jnp.concatenate([got[...] for got in (in_a, in_b, in_c, in_d)], axis=0)
    spots = [sent_rows(meta, n, h) for n in range(4) for h in range(HB)]
    rows_of = jnp.concatenate([dense[at, ROWS:ROWS + HALO] for at in spots], axis=0)
    product = dot(rows_of, halo)
    for n, at in enumerate(spots):
        here = slice(n * ORB, (n + 1) * ORB)
        out = outs[n // HB]
        out[n % HB * ORB:(n % HB + 1) * ORB, :] = (base[at, :] + scale * product[here, :]).astype(BF16)


def step_kernel(scale, in_a, in_b, in_c, in_d, dense, base, before, new_base, cur, halo, low):
    for n, got in enumerate((in_a, in_b, in_c, in_d)):
        halo[n * 2 * ORB:(n + 1) * 2 * ORB, :] = got[...]
    for m in range(ROWS // MT):
        rows = slice(m * MT, (m + 1) * MT)
        value = base[rows, :] + scale * dot(dense[rows, ROWS:ROWS + HALO], halo[...])
        cur[rows, :] = value
        low[rows, :] = value.astype(BF16)
    for m in range(ROWS // MT):
        rows = slice(m * MT, (m + 1) * MT)
        product = dot(dense[rows, :ROWS], low[...])
        new_base[rows, :] = (
            (2.0 / HALF_WIDTH) * product
            - (2.0 * SHIFT / HALF_WIDTH) * cur[rows, :]
            - before[rows, :]
        )


def last_kernel(scale, weight, in_a, in_b, in_c, in_d, dense, base, rotation, rotated, margin, halo, total):
    for n, got in enumerate((in_a, in_b, in_c, in_d)):
        halo[n * 2 * ORB:(n + 1) * 2 * ORB, :] = got[...]
    for m in range(ROWS // MT):
        rows = slice(m * MT, (m + 1) * MT)
        value = base[rows, :] + scale * dot(dense[rows, ROWS:ROWS + HALO], halo[...])
        turned = dot(value.astype(BF16), rotation[...]).astype(BF16)
        rotated[rows, :] = turned
        share = lax.dot_general(turned, turned, (((0,), (0,)), ((), ())), preferred_element_type=F32)
        total[...] = share if m == 0 else total[...] + share
    margin[...] = (total[...] * weight).reshape(SUB, 2, SUB // 2).astype(BF16)


def sum_kernel(parts, out):
    total = jnp.sum(parts[...].astype(F32), axis=0)
    for n in range(2):
        out[:, n * 128:(n + 1) * 128] = total[n:n + 1, :]


def params(**kw):
    return pltpu.CompilerParams(vmem_limit_bytes=16 * 1024 * 1024, **kw)


def cost(flops):
    return pl.CostEstimate(flops=int(flops), bytes_accessed=4 << 20, transcendentals=0)


V = pl.BlockSpec(memory_space=VMEM)
S = pl.BlockSpec(memory_space=SMEM)
H = pl.BlockSpec(memory_space=pltpu.HBM)


def on_device(pairs, subspace, hamiltonian, neighbours, send_lists, rotation):
    ham = hamiltonian.reshape(ROWS, NB * ORB)
    nbr = neighbours.reshape(BLK, NB).T
    lists = send_lists.reshape(4, HB).T
    sub = subspace.reshape(ROWS, SUB)
    ham, sub, nbr = [pltpu.with_memory_space_constraint(x, pltpu.HBM) for x in (ham, sub, nbr)]
    size_x, size_y = lax.axis_size("gx"), lax.axis_size("gy")
    packet = VMEM((2 * ORB, SUB), BF16)
    field = VMEM((ROWS, SUB), F32)
    halo = VMEM((HALO, SUB), BF16)

    def swap(packets):
        return [lax.ppermute(packets[n], ("gx", "gy"), pairs[n]) for n in range(4)]

    table = VMEM((ROWS, WIDE), BF16)
    *packets, meta, nbr, ham, sub, dense = pl.pallas_call(
        functools.partial(first_kernel, (size_x - 1, size_y - 1)),
        out_shape=[packet] * 4 + [
            SMEM((4 + 4 * HB,), jnp.int32), SMEM(nbr.shape, jnp.int32), VMEM(ham.shape, BF16), VMEM(sub.shape, BF16), table
        ],
        in_specs=[S, H, H, H],
        out_specs=[V] * 4 + [S, S, V, V, V],
        scratch_shapes=[pltpu.SemaphoreType.DMA((4 * HB + 3,))],
        compiler_params=params(),
        name="first",
    )(lists, nbr, ham, sub)
    received = swap(packets)
    dense, base, *cur = pl.pallas_call(
        build_kernel,
        out_shape=[table, field, field],
        in_specs=[S, S, V, V, V],
        out_specs=[V] * 3,
        input_output_aliases={4: 0},
        scratch_shapes=[SMEM((SPARE + 8,), jnp.int32)],
        compiler_params=params(),
        cost_estimate=cost(2e9),
        name="build_and_local",
    )(meta, nbr, ham, sub, dense)
    for step in range(1, STEPS):
        scale = (1.0 if step == 1 else 2.0) / HALF_WIDTH
        packets = pl.pallas_call(
            functools.partial(packets_kernel, scale),
            out_shape=[packet] * 4,
            in_specs=[S] + [V] * 6,
            out_specs=[V] * 4,
            compiler_params=params(),
            name="packets",
        )(meta, *received, dense, base)
        landed = received
        received = swap(packets)
        keep = step < STEPS - 1
        fields = [VMEM((ROWS, SUB), F32)] * (2 if keep else 1)
        base, *cur = pl.pallas_call(
            functools.partial(step_kernel, scale),
            out_shape=fields,
            in_specs=[V] * 7,
            out_specs=[V] * len(fields),
            scratch_shapes=([] if keep else [field]) + [halo, VMEM((ROWS, SUB), BF16)],
            compiler_params=params(),
            cost_estimate=cost(2.7e9),
            name="step",
        )(*landed, dense, base, *cur)
    orbitals = ROWS * size_x * size_y
    rotated, share = pl.pallas_call(
        functools.partial(last_kernel, 2.0 / HALF_WIDTH, 1.0 / orbitals),
        out_shape=[VMEM((ROWS, SUB), BF16), VMEM((SUB, 2, SUB // 2), BF16)],
        in_specs=[V] * 7,
        out_specs=[V] * 2,
        scratch_shapes=[halo, VMEM((SUB, SUB), F32)],
        compiler_params=params(),
        name="last",
    )(*received, dense, base, rotation)
    parts = lax.all_to_all(share, ("gx", "gy"), 0, 0, tiled=True)
    margin = pl.pallas_call(
        sum_kernel,
        out_shape=jax.ShapeDtypeStruct((1, SUB), F32),
        in_specs=[V],
        out_specs=V,
        compiler_params=params(),
        name="sum_parts",
    )(parts)
    return rotated.reshape(subspace.shape), margin


def solution(mesh):
    pairs = exchange_pairs((mesh.shape["gx"], mesh.shape["gy"]))
    return jax.shard_map(
        functools.partial(on_device, pairs),
        mesh=mesh,
        in_specs=(
            P("gx", "gy", None, None),
            P("gx", "gy", None, None, None),
            P("gx", "gy", None, None),
            P("gx", "gy", None, None),
            P(),
        ),
        out_specs=(P("gx", "gy", None, None), P(("gx", "gy"), None)),
        check_vma=False,
    )
```

```python
import functools

import jax
import jax.numpy as jnp
from jax import lax
from jax.experimental import pallas as pl
from jax.experimental.pallas import tpu as pltpu
from jax.sharding import PartitionSpec as P

STEPS = 6
SHIFT = 0.1
HALF_WIDTH = 0.8

F32 = jnp.float32
BF16 = jnp.bfloat16
VMEM = pltpu.VMEM
SMEM = pltpu.SMEM

ORB = 64
NB = 8
BLK = 32
HB = 2
ROWS = BLK * ORB
SUB = 256
HALO = 4 * HB * ORB
WIDE = ROWS + HALO + 2 * ORB
SPARE = BLK + 4 * HB
MT = 512
GROUP = 4


SWAPS = ((0, 1), (1, 1), (1, 0), (0, 0))


def exchange_pairs(tiles):
    grid = [(i, j) for i in range(tiles[0]) for j in range(tiles[1])]

    def partner(spot, axis, outer):
        place = list(spot)
        if outer and place[axis] in (0, tiles[axis] - 1):
            place[1 - axis] ^= 1
        else:
            place[axis] = ((place[axis] - outer) ^ 1) + outer
        return place[0] * tiles[1] + place[1]

    return [[(i * tiles[1] + j, partner((i, j), *swap)) for i, j in grid] for swap in SWAPS]


def dot(a, b):
    return jnp.dot(a, b, preferred_element_type=F32)


def build_kernel(meta, nbr, ham, sub, cleared, dense, base, cur, remap):
    for s in range(BLK):
        remap[s] = jnp.int32(s)
    for axis in range(2):
        pos, last = meta[axis], meta[2 + axis]
        even = (pos & 1) == 0
        inner, outer = SWAPS.index((axis, 0)), SWAPS.index((axis, 1))
        before, after = jnp.where(even, outer, inner), jnp.where(even, inner, outer)
        for h in range(HB):
            s = BLK + 2 * axis * HB + h
            remap[s] = jnp.where(pos > 0, BLK + before * HB + h, SPARE)
            remap[s + HB] = jnp.where(pos < last, BLK + after * HB + h, SPARE)

    low = lax.broadcasted_iota(jnp.int32, (ORB, 2 * ORB), 1) < ORB
    keep_low = jnp.where(low, 1.0, 0.0).astype(BF16)
    keep_high = jnp.where(low, 0.0, 1.0).astype(BF16)

    def group(g, carry):
        rows = [pl.ds(pl.multiple_of((g * GROUP + n) * ORB, ORB), ORB) for n in range(GROUP)]
        for kk in range(NB // 2):
            tiles = [ham[rows[n], kk * 128:(kk + 1) * 128] for n in range(GROUP)]
            for e in range(2):
                spots, values = [], []
                for n in range(GROUP):
                    s = remap[nbr[2 * kk + e, g * GROUP + n]]
                    half = tiles[n] * (keep_low if e == 0 else keep_high)
                    piece = pltpu.roll(half, jnp.where((s & 1) == e, 0, ORB), 1)
                    spots.append((rows[n], pl.ds(pl.multiple_of((s >> 1) * 128, 128), 128)))
                    values.append(dense[spots[n]] + piece)
                for n in range(GROUP):
                    dense[spots[n]] = values[n]
        return carry

    lax.fori_loop(0, BLK // GROUP, group, 0)
    for m in range(ROWS // MT):
        rows = slice(m * MT, (m + 1) * MT)
        wide = sub[rows, :].astype(F32)
        cur[rows, :] = wide
        product = dot(dense[rows, :ROWS], sub[...])
        base[rows, :] = (1.0 / HALF_WIDTH) * product - (SHIFT / HALF_WIDTH) * wide


def sent_rows(meta, n, h):
    axis, outer = SWAPS[n]
    packet = 2 * axis + ((meta[axis] + outer) & 1)
    return pl.ds(pl.multiple_of(meta[4 + h * 4 + packet] * ORB, ORB), ORB)


def first_kernel(limits, lists, nbr_hbm, ham_hbm, sub_hbm, out_a, out_b, out_c, out_d, meta, nbr, ham, sub, dense, sems):
    for axis, name in enumerate(("gx", "gy")):
        meta[axis] = lax.axis_index(name)
        meta[2 + axis] = jnp.int32(limits[axis])
    for n in range(4):
        for h in range(HB):
            meta[4 + h * 4 + n] = lists[h, n]
    copies = []
    for n, out in enumerate((out_a, out_b, out_c, out_d)):
        for h in range(HB):
            copies.append((sub_hbm.at[sent_rows(meta, n, h), :], out.at[pl.ds(h * ORB, ORB), :]))
    copies += [(nbr_hbm, nbr), (ham_hbm, ham), (sub_hbm, sub)]
    copies = [pltpu.make_async_copy(*pair, sems.at[n]) for n, pair in enumerate(copies)]
    for copy in copies:
        copy.start()

    def clear(m, carry):
        dense[pl.ds(pl.multiple_of(m * ORB, ORB), ORB), :ROWS + HALO] = jnp.zeros((ORB, ROWS + HALO), BF16)
        return carry

    lax.fori_loop(0, BLK, clear, 0)
    for copy in copies:
        copy.wait()


def packets_kernel(scale, meta, in_a, in_b, in_c, in_d, dense, base, out_a, out_b, out_c, out_d):
    outs = (out_a, out_b, out_c, out_d)
    halo = jnp.concatenate([got[...] for got in (in_a, in_b, in_c, in_d)], axis=0)
    spots = [sent_rows(meta, n, h) for n in range(4) for h in range(HB)]
    rows_of = jnp.concatenate([dense[at, ROWS:ROWS + HALO] for at in spots], axis=0)
    product = dot(rows_of, halo)
    for n, at in enumerate(spots):
        here = slice(n * ORB, (n + 1) * ORB)
        out = outs[n // HB]
        out[n % HB * ORB:(n % HB + 1) * ORB, :] = (base[at, :] + scale * product[here, :]).astype(BF16)


def step_kernel(scale, in_a, in_b, in_c, in_d, dense, base, before, new_base, cur, halo, low):
    for n, got in enumerate((in_a, in_b, in_c, in_d)):
        halo[n * 2 * ORB:(n + 1) * 2 * ORB, :] = got[...]
    for m in range(ROWS // MT):
        rows = slice(m * MT, (m + 1) * MT)
        value = base[rows, :] + scale * dot(dense[rows, ROWS:ROWS + HALO], halo[...])
        cur[rows, :] = value
        low[rows, :] = value.astype(BF16)
    for m in range(ROWS // MT):
        rows = slice(m * MT, (m + 1) * MT)
        product = dot(dense[rows, :ROWS], low[...])
        new_base[rows, :] = (
            (2.0 / HALF_WIDTH) * product
            - (2.0 * SHIFT / HALF_WIDTH) * cur[rows, :]
            - before[rows, :]
        )


def last_kernel(scale, weight, in_a, in_b, in_c, in_d, dense, base, rotation, filtered, margin, halo, gram):
    for n, got in enumerate((in_a, in_b, in_c, in_d)):
        halo[n * 2 * ORB:(n + 1) * 2 * ORB, :] = got[...]
    for m in range(ROWS // MT):
        rows = slice(m * MT, (m + 1) * MT)
        value = base[rows, :] + scale * dot(dense[rows, ROWS:ROWS + HALO], halo[...])
        low = value.astype(BF16)
        filtered[rows, :] = low
        part = across(low, low)
        gram[...] = part if m == 0 else gram[...] + part
    high, rest = split(gram[...])
    right = dot(high, rotation[...]) + dot(rest, rotation[...])
    high, rest = split(right)
    total = across(rotation[...], high) + across(rotation[...], rest)
    margin[...] = (total * weight).reshape(SUB, 2, SUB // 2).astype(BF16)


def across(a, b):
    return lax.dot_general(a, b, (((0,), (0,)), ((), ())), preferred_element_type=F32)


def split(value):
    high = value.astype(BF16)
    return high, (value - high.astype(F32)).astype(BF16)


def rotate_kernel(filtered, rotation, rotated):
    for m in range(ROWS // MT):
        rows = slice(m * MT, (m + 1) * MT)
        rotated[rows, :] = dot(filtered[rows, :], rotation[...]).astype(BF16)


def sum_kernel(parts, out):
    total = parts[0:8].astype(F32)
    for n in range(8, parts.shape[0], 8):
        total = total + parts[n:n + 8].astype(F32)
    total = jnp.sum(total, axis=0)
    for n in range(2):
        out[:, n * 128:(n + 1) * 128] = total[n:n + 1, :]


def params(**kw):
    return pltpu.CompilerParams(vmem_limit_bytes=16 * 1024 * 1024, **kw)


def cost(flops):
    return pl.CostEstimate(flops=int(flops), bytes_accessed=4 << 20, transcendentals=0)


V = pl.BlockSpec(memory_space=VMEM)
S = pl.BlockSpec(memory_space=SMEM)
H = pl.BlockSpec(memory_space=pltpu.HBM)


def on_device(pairs, subspace, hamiltonian, neighbours, send_lists, rotation):
    ham = hamiltonian.reshape(ROWS, NB * ORB)
    nbr = neighbours.reshape(BLK, NB).T
    lists = send_lists.reshape(4, HB).T
    sub = subspace.reshape(ROWS, SUB)
    ham, sub, nbr, lists = [pltpu.with_memory_space_constraint(x, pltpu.HBM) for x in (ham, sub, nbr, lists)]
    size_x, size_y = lax.axis_size("gx"), lax.axis_size("gy")
    packet = VMEM((2 * ORB, SUB), BF16)
    field = VMEM((ROWS, SUB), F32)
    halo = VMEM((HALO, SUB), BF16)

    def swap(packets):
        return [lax.ppermute(packets[n], ("gx", "gy"), pairs[n]) for n in range(4)]

    table = VMEM((ROWS, WIDE), BF16)
    *packets, meta, nbr, ham, sub, dense = pl.pallas_call(
        functools.partial(first_kernel, (size_x - 1, size_y - 1)),
        out_shape=[packet] * 4 + [
            SMEM((4 + 4 * HB,), jnp.int32), SMEM(nbr.shape, jnp.int32), VMEM(ham.shape, BF16), VMEM(sub.shape, BF16), table
        ],
        in_specs=[S, H, H, H],
        out_specs=[V] * 4 + [S, S, V, V, V],
        scratch_shapes=[pltpu.SemaphoreType.DMA((4 * HB + 3,))],
        compiler_params=params(),
        name="first",
    )(lists, nbr, ham, sub)
    received = swap(packets)
    dense, base, *cur = pl.pallas_call(
        build_kernel,
        out_shape=[table, field, field],
        in_specs=[S, S, V, V, V],
        out_specs=[V] * 3,
        input_output_aliases={4: 0},
        scratch_shapes=[SMEM((SPARE + 8,), jnp.int32)],
        compiler_params=params(),
        cost_estimate=cost(2e9),
        name="build_and_local",
    )(meta, nbr, ham, sub, dense)
    for step in range(1, STEPS):
        scale = (1.0 if step == 1 else 2.0) / HALF_WIDTH
        packets = pl.pallas_call(
            functools.partial(packets_kernel, scale),
            out_shape=[packet] * 4,
            in_specs=[S] + [V] * 6,
            out_specs=[V] * 4,
            compiler_params=params(),
            name="packets",
        )(meta, *received, dense, base)
        landed = received
        received = swap(packets)
        keep = step < STEPS - 1
        fields = [VMEM((ROWS, SUB), F32)] * (2 if keep else 1)
        base, *cur = pl.pallas_call(
            functools.partial(step_kernel, scale),
            out_shape=fields,
            in_specs=[V] * 7,
            out_specs=[V] * len(fields),
            scratch_shapes=([] if keep else [field]) + [halo, VMEM((ROWS, SUB), BF16)],
            compiler_params=params(),
            cost_estimate=cost(2.7e9),
            name="step",
        )(*landed, dense, base, *cur)
    orbitals = ROWS * size_x * size_y
    filtered, share = pl.pallas_call(
        functools.partial(last_kernel, 2.0 / HALF_WIDTH, 1.0 / orbitals),
        out_shape=[VMEM((ROWS, SUB), BF16), VMEM((SUB, 2, SUB // 2), BF16)],
        in_specs=[V] * 7,
        out_specs=[V] * 2,
        scratch_shapes=[halo, VMEM((SUB, SUB), F32)],
        compiler_params=params(),
        name="last",
    )(*received, dense, base, rotation)
    parts = lax.all_to_all(share, ("gx", "gy"), 0, 0, tiled=True)
    rotated = pl.pallas_call(
        rotate_kernel,
        out_shape=jax.ShapeDtypeStruct((ROWS, SUB), BF16),
        in_specs=[V] * 2,
        out_specs=V,
        compiler_params=params(),
        cost_estimate=cost(2.7e8),
        name="rotate",
    )(filtered, rotation)
    margin = pl.pallas_call(
        sum_kernel,
        out_shape=jax.ShapeDtypeStruct((1, SUB), F32),
        in_specs=[V],
        out_specs=V,
        compiler_params=params(),
        name="sum_parts",
    )(parts)
    return rotated.reshape(subspace.shape), margin


def solution(mesh):
    pairs = exchange_pairs((mesh.shape["gx"], mesh.shape["gy"]))
    return jax.shard_map(
        functools.partial(on_device, pairs),
        mesh=mesh,
        in_specs=(
            P("gx", "gy", None, None),
            P("gx", "gy", None, None, None),
            P("gx", "gy", None, None),
            P("gx", "gy", None, None),
            P(),
        ),
        out_specs=(P("gx", "gy", None, None), P(("gx", "gy"), None)),
        check_vma=False,
    )
```

```python
import functools

import jax
import jax.numpy as jnp
from jax import lax
from jax.experimental import pallas as pl
from jax.experimental.pallas import tpu as pltpu
from jax.sharding import PartitionSpec as P

STEPS = 6
SHIFT = 0.1
HALF_WIDTH = 0.8

F32 = jnp.float32
BF16 = jnp.bfloat16
VMEM = pltpu.VMEM
SMEM = pltpu.SMEM

ORB = 64
NB = 8
BLK = 32
HB = 2
ROWS = BLK * ORB
SUB = 256
HALO = 4 * HB * ORB
WIDE = ROWS + HALO + 2 * ORB
SPARE = BLK + 4 * HB
MT = 512
GROUP = 4


SWAPS = ((0, 1), (1, 1), (1, 0), (0, 0))


def exchange_pairs(tiles):
    grid = [(i, j) for i in range(tiles[0]) for j in range(tiles[1])]

    def partner(spot, axis, outer):
        place = list(spot)
        if outer and place[axis] in (0, tiles[axis] - 1):
            place[1 - axis] ^= 1
        else:
            place[axis] = ((place[axis] - outer) ^ 1) + outer
        return place[0] * tiles[1] + place[1]

    return [[(i * tiles[1] + j, partner((i, j), *swap)) for i, j in grid] for swap in SWAPS]


def dot(a, b):
    return jnp.dot(a, b, preferred_element_type=F32)


def build_kernel(remap, nbr, ham, sub, cleared, dense, base, cur):
    low = lax.broadcasted_iota(jnp.int32, (ORB, 2 * ORB), 1) < ORB
    keep_low = jnp.where(low, 1.0, 0.0).astype(BF16)
    keep_high = jnp.where(low, 0.0, 1.0).astype(BF16)

    def group(g, carry):
        rows = [pl.ds(pl.multiple_of((g * GROUP + n) * ORB, ORB), ORB) for n in range(GROUP)]
        for kk in range(NB // 2):
            tiles = [ham[rows[n], kk * 128:(kk + 1) * 128] for n in range(GROUP)]
            for e in range(2):
                spots, values = [], []
                for n in range(GROUP):
                    s = remap[nbr[2 * kk + e, g * GROUP + n]]
                    half = tiles[n] * (keep_low if e == 0 else keep_high)
                    piece = pltpu.roll(half, jnp.where((s & 1) == e, 0, ORB), 1)
                    spots.append((rows[n], pl.ds(pl.multiple_of((s >> 1) * 128, 128), 128)))
                    values.append(dense[spots[n]] + piece)
                for n in range(GROUP):
                    dense[spots[n]] = values[n]
        return carry

    lax.fori_loop(0, BLK // GROUP, group, 0)
    for m in range(ROWS // MT):
        rows = slice(m * MT, (m + 1) * MT)
        wide = sub[rows, :].astype(F32)
        cur[rows, :] = wide
        product = dot(dense[rows, :ROWS], sub[...])
        base[rows, :] = (1.0 / HALF_WIDTH) * product - (SHIFT / HALF_WIDTH) * wide


def sent_rows(meta, n, h):
    axis, outer = SWAPS[n]
    packet = 2 * axis + ((meta[axis] + outer) & 1)
    return pl.ds(pl.multiple_of(meta[4 + h * 4 + packet] * ORB, ORB), ORB)


def first_kernel(limits, lists, nbr_hbm, ham_hbm, sub_hbm, out_a, out_b, out_c, out_d, meta, remap, nbr, ham, sub, dense, sems):
    for axis, name in enumerate(("gx", "gy")):
        meta[axis] = lax.axis_index(name)
        meta[2 + axis] = jnp.int32(limits[axis])
    for n in range(4):
        for h in range(HB):
            meta[4 + h * 4 + n] = lists[h, n]
    copies = []
    for n, out in enumerate((out_a, out_b, out_c, out_d)):
        for h in range(HB):
            copies.append((sub_hbm.at[sent_rows(meta, n, h), :], out.at[pl.ds(h * ORB, ORB), :]))
    copies += [(nbr_hbm, nbr), (ham_hbm, ham), (sub_hbm, sub)]
    copies = [pltpu.make_async_copy(*pair, sems.at[n]) for n, pair in enumerate(copies)]
    for copy in copies:
        copy.start()

    for s in range(BLK):
        remap[s] = jnp.int32(s)
    for axis in range(2):
        pos, last = meta[axis], meta[2 + axis]
        even = (pos & 1) == 0
        inner, outer = SWAPS.index((axis, 0)), SWAPS.index((axis, 1))
        before, after = jnp.where(even, outer, inner), jnp.where(even, inner, outer)
        for h in range(HB):
            s = BLK + 2 * axis * HB + h
            remap[s] = jnp.where(pos > 0, BLK + before * HB + h, SPARE)
            remap[s + HB] = jnp.where(pos < last, BLK + after * HB + h, SPARE)

    def clear(m, carry):
        dense[pl.ds(pl.multiple_of(m * ORB, ORB), ORB), :ROWS + HALO] = jnp.zeros((ORB, ROWS + HALO), BF16)
        return carry

    lax.fori_loop(0, BLK, clear, 0)
    for copy in copies:
        copy.wait()


def packets_kernel(scale, meta, in_a, in_b, in_c, in_d, dense, base, out_a, out_b, out_c, out_d):
    outs = (out_a, out_b, out_c, out_d)
    halo = jnp.concatenate([got[...] for got in (in_a, in_b, in_c, in_d)], axis=0)
    spots = [sent_rows(meta, n, h) for n in range(4) for h in range(HB)]
    rows_of = jnp.concatenate([dense[at, ROWS:ROWS + HALO] for at in spots], axis=0)
    product = dot(rows_of, halo)
    for n, at in enumerate(spots):
        here = slice(n * ORB, (n + 1) * ORB)
        out = outs[n // HB]
        out[n % HB * ORB:(n % HB + 1) * ORB, :] = (base[at, :] + scale * product[here, :]).astype(BF16)


def step_kernel(scale, in_a, in_b, in_c, in_d, dense, base, before, new_base, cur, halo, low):
    for n, got in enumerate((in_a, in_b, in_c, in_d)):
        halo[n * 2 * ORB:(n + 1) * 2 * ORB, :] = got[...]
    for m in range(ROWS // MT):
        rows = slice(m * MT, (m + 1) * MT)
        value = base[rows, :] + scale * dot(dense[rows, ROWS:ROWS + HALO], halo[...])
        cur[rows, :] = value
        low[rows, :] = value.astype(BF16)
    for m in range(ROWS // MT):
        rows = slice(m * MT, (m + 1) * MT)
        product = dot(dense[rows, :ROWS], low[...])
        new_base[rows, :] = (
            (2.0 / HALF_WIDTH) * product
            - (2.0 * SHIFT / HALF_WIDTH) * cur[rows, :]
            - before[rows, :]
        )


def last_kernel(scale, weight, in_a, in_b, in_c, in_d, dense, base, rotation, filtered, margin, halo, gram):
    for n, got in enumerate((in_a, in_b, in_c, in_d)):
        halo[n * 2 * ORB:(n + 1) * 2 * ORB, :] = got[...]
    for m in range(ROWS // MT):
        rows = slice(m * MT, (m + 1) * MT)
        value = base[rows, :] + scale * dot(dense[rows, ROWS:ROWS + HALO], halo[...])
        low = value.astype(BF16)
        filtered[rows, :] = low
        part = across(low, low)
        gram[...] = part if m == 0 else gram[...] + part
    high, rest = split(gram[...])
    right = dot(high, rotation[...]) + dot(rest, rotation[...])
    high, rest = split(right)
    total = across(rotation[...], high) + across(rotation[...], rest)
    margin[...] = (total * weight).reshape(SUB, 2, SUB // 2).astype(BF16)


def across(a, b):
    return lax.dot_general(a, b, (((0,), (0,)), ((), ())), preferred_element_type=F32)


def split(value):
    high = value.astype(BF16)
    return high, (value - high.astype(F32)).astype(BF16)


def rotate_kernel(filtered, rotation, rotated):
    for m in range(ROWS // MT):
        rows = slice(m * MT, (m + 1) * MT)
        rotated[rows, :] = dot(filtered[rows, :], rotation[...]).astype(BF16)


def sum_kernel(parts, out):
    total = parts[0:8].astype(F32)
    for n in range(8, parts.shape[0], 8):
        total = total + parts[n:n + 8].astype(F32)
    total = jnp.sum(total, axis=0)
    for n in range(2):
        out[:, n * 128:(n + 1) * 128] = total[n:n + 1, :]


def params(**kw):
    return pltpu.CompilerParams(vmem_limit_bytes=16 * 1024 * 1024, **kw)


def cost(flops):
    return pl.CostEstimate(flops=int(flops), bytes_accessed=4 << 20, transcendentals=0)


V = pl.BlockSpec(memory_space=VMEM)
S = pl.BlockSpec(memory_space=SMEM)
H = pl.BlockSpec(memory_space=pltpu.HBM)


def on_device(pairs, subspace, hamiltonian, neighbours, send_lists, rotation):
    ham = hamiltonian.reshape(ROWS, NB * ORB)
    nbr = neighbours.reshape(BLK, NB).T
    lists = send_lists.reshape(4, HB).T
    sub = subspace.reshape(ROWS, SUB)
    ham, sub, nbr, lists = [pltpu.with_memory_space_constraint(x, pltpu.HBM) for x in (ham, sub, nbr, lists)]
    size_x, size_y = lax.axis_size("gx"), lax.axis_size("gy")
    packet = VMEM((2 * ORB, SUB), BF16)
    field = VMEM((ROWS, SUB), F32)
    halo = VMEM((HALO, SUB), BF16)

    def swap(packets):
        return [lax.ppermute(packets[n], ("gx", "gy"), pairs[n]) for n in range(4)]

    table = VMEM((ROWS, WIDE), BF16)
    *packets, meta, remap, nbr, ham, sub, dense = pl.pallas_call(
        functools.partial(first_kernel, (size_x - 1, size_y - 1)),
        out_shape=[packet] * 4 + [
            SMEM((4 + 4 * HB,), jnp.int32), SMEM((SPARE + 8,), jnp.int32), SMEM(nbr.shape, jnp.int32),
            VMEM(ham.shape, BF16), VMEM(sub.shape, BF16), table
        ],
        in_specs=[S, H, H, H],
        out_specs=[V] * 4 + [S, S, S, V, V, V],
        scratch_shapes=[pltpu.SemaphoreType.DMA((4 * HB + 3,))],
        compiler_params=params(),
        name="first",
    )(lists, nbr, ham, sub)
    received = swap(packets)
    dense, base, *cur = pl.pallas_call(
        build_kernel,
        out_shape=[table, field, field],
        in_specs=[S, S, V, V, V],
        out_specs=[V] * 3,
        input_output_aliases={4: 0},
        compiler_params=params(),
        cost_estimate=cost(2e9),
        name="build_and_local",
    )(remap, nbr, ham, sub, dense)
    for step in range(1, STEPS):
        scale = (1.0 if step == 1 else 2.0) / HALF_WIDTH
        packets = pl.pallas_call(
            functools.partial(packets_kernel, scale),
            out_shape=[packet] * 4,
            in_specs=[S] + [V] * 6,
            out_specs=[V] * 4,
            compiler_params=params(),
            name="packets",
        )(meta, *received, dense, base)
        landed = received
        received = swap(packets)
        keep = step < STEPS - 1
        fields = [VMEM((ROWS, SUB), F32)] * (2 if keep else 1)
        base, *cur = pl.pallas_call(
            functools.partial(step_kernel, scale),
            out_shape=fields,
            in_specs=[V] * 7,
            out_specs=[V] * len(fields),
            scratch_shapes=([] if keep else [field]) + [halo, VMEM((ROWS, SUB), BF16)],
            compiler_params=params(),
            cost_estimate=cost(2.7e9),
            name="step",
        )(*landed, dense, base, *cur)
    orbitals = ROWS * size_x * size_y
    filtered, share = pl.pallas_call(
        functools.partial(last_kernel, 2.0 / HALF_WIDTH, 1.0 / orbitals),
        out_shape=[VMEM((ROWS, SUB), BF16), VMEM((SUB, 2, SUB // 2), BF16)],
        in_specs=[V] * 7,
        out_specs=[V] * 2,
        scratch_shapes=[halo, VMEM((SUB, SUB), F32)],
        compiler_params=params(),
        name="last",
    )(*received, dense, base, rotation)
    parts = lax.all_to_all(share, ("gx", "gy"), 0, 0, tiled=True)
    rotated = pl.pallas_call(
        rotate_kernel,
        out_shape=jax.ShapeDtypeStruct((ROWS, SUB), BF16),
        in_specs=[V] * 2,
        out_specs=V,
        compiler_params=params(),
        cost_estimate=cost(2.7e8),
        name="rotate",
    )(filtered, rotation)
    margin = pl.pallas_call(
        sum_kernel,
        out_shape=jax.ShapeDtypeStruct((1, SUB), F32),
        in_specs=[V],
        out_specs=V,
        compiler_params=params(),
        name="sum_parts",
    )(parts)
    return rotated.reshape(subspace.shape), margin


def solution(mesh):
    pairs = exchange_pairs((mesh.shape["gx"], mesh.shape["gy"]))
    return jax.shard_map(
        functools.partial(on_device, pairs),
        mesh=mesh,
        in_specs=(
            P("gx", "gy", None, None),
            P("gx", "gy", None, None, None),
            P("gx", "gy", None, None),
            P("gx", "gy", None, None),
            P(),
        ),
        out_specs=(P("gx", "gy", None, None), P(("gx", "gy"), None)),
        check_vma=False,
    )
```
